1024 devices in a mesh: row: 32 (over x_hi, z), col: 32 (over x_lo, y, core).
Axes of the slice: x: 4 (x_hi: 2, x_lo: 2; x = x_hi * 2 + x_lo), y: 8, z: 16, core: 2. Of those that a mesh axis runs over, the one named last changes fastest.
Arguments:
- inputs: bfloat16 [128, 12288], P('col', 'row'), may hold values from -6 to 6
- weight_in: bfloat16 [12288, 24576], P('row', 'col'), may hold values from -0.0546875 to 0.0546875
- weight_out: bfloat16 [24576, 12288], P('col', 'row'), may hold values from -0.0390625 to 0.0390625
- grad_out: bfloat16 [128, 12288], P('col', 'row'), may hold values from -0.8984375 to 0.8984375
Outputs:
- block_out: bfloat16 [128, 12288], P('col', 'row')
- grad_inputs: bfloat16 [128, 12288], P('col', 'row')
- grad_weight_in: bfloat16 [12288, 24576], P('row', 'col')
- grad_weight_out: bfloat16 [24576, 12288], P('col', 'row')
The draws below stay inside these ranges and needn't reach their ends.
All inputs are finite; a program needn't handle non-finite values.
Results may differ from the reference program's by a relative error of at most 0.0061.
Values may be sent and summed in bfloat16 or wider, within the bound.
A program may use at most 32 MiB of HBM per device.

```python
import math
import jax
import jax.numpy as jnp

D = 12288
FF = 24576
TOKENS = 128


def shard_levels(own_key, shape, pieces, smallest, top_value):
    loudness = 1.0
    for position, parts in pieces:
        heights = jax.random.uniform(jax.random.fold_in(jax.random.fold_in(own_key, 6), position), (parts,), jnp.float32, smallest / len(pieces), top_value / len(pieces))
        loudness = loudness * jnp.repeat(jnp.exp(heights), shape[position] // parts).reshape((-1,) + (1,) * (len(shape) - 1 - position))
    return loudness


def bell_draw(key, shape, deviation, bound, cuts=(), kind=jnp.bfloat16):
    level = shard_levels(key, shape, cuts, -0.22, 0.18) if cuts else 1.0
    drawn = jax.random.normal(key, shape, jnp.float32) * deviation * level
    return jnp.minimum(jnp.maximum(drawn, -bound), bound).astype(kind)


def setup_inputs(seed: int = 0) -> dict:
    key_of = jax.random.split(jax.random.key(seed), 5)
    return {
        "inputs": bell_draw(key_of[0], (TOKENS, D), 1.0, 6.0, ((0, 32), (1, 32))),
        "weight_in": bell_draw(key_of[1], (D, FF), D ** -0.5, 0.0546875, ((0, 32), (1, 32))),
        "weight_out": bell_draw(key_of[2], (FF, D), FF ** -0.5, 0.0390625, ((0, 32), (1, 32))),
        "grad_out": bell_draw(key_of[3], (TOKENS, D), 0.15, 0.8984375, ((0, 32), (1, 32))),
    }


gelu_coef = math.sqrt(2.0 / math.pi)

def gelu_value(value):
    inner = gelu_coef * (value + 0.044715 * value * value * value)
    return 0.5 * value * (1.0 + jnp.tanh(inner))

def gelu_slope(value):
    inner = gelu_coef * (value + 0.044715 * value * value * value)
    tanh_value = jnp.tanh(inner)
    return 0.5 * (1.0 + tanh_value) + 0.5 * value * (1.0 - tanh_value * tanh_value) * gelu_coef * (1.0 + 3.0 * 0.044715 * value * value)

def reference(inputs, weight_in, weight_out, grad_out):
    pre_gelu = jnp.dot(inputs, weight_in, preferred_element_type=jnp.float32).astype(jnp.bfloat16)
    pre_float = pre_gelu.astype(jnp.float32)
    activation = gelu_value(pre_float).astype(jnp.bfloat16)
    block_out = jnp.dot(activation, weight_out, preferred_element_type=jnp.float32).astype(jnp.bfloat16)
    grad_weight_out = jnp.dot(activation.T, grad_out, preferred_element_type=jnp.float32).astype(jnp.bfloat16)
    grad_activation = jnp.dot(grad_out, weight_out.T, preferred_element_type=jnp.float32)
    grad_pre_gelu = (grad_activation * gelu_slope(pre_float)).astype(jnp.bfloat16)
    grad_weight_in = jnp.dot(inputs.T, grad_pre_gelu, preferred_element_type=jnp.float32).astype(jnp.bfloat16)
    grad_inputs = jnp.dot(grad_pre_gelu, weight_in.T, preferred_element_type=jnp.float32).astype(jnp.bfloat16)
    return (block_out, grad_inputs, grad_weight_in, grad_weight_out)
```

```python
import functools
import math

import jax
import jax.numpy as jnp
from jax import lax
from jax.experimental import pallas as pl
from jax.experimental.pallas import tpu as pltpu
from jax.sharding import PartitionSpec as P

MESH = pl.DeviceIdType.MESH
F32, BF16 = jnp.float32, jnp.bfloat16
gelu_coef = math.sqrt(2.0 / math.pi)
Z, Y = 16, 8

row_offsets = sorted(
    [(h, k) for h in range(2) for k in range(Z) if (h, k) != (0, 0)],
    key=lambda t: -(min(t[1], Z - t[1]) + 2 * t[0]),
)
chip_offsets = sorted(
    [(h, k) for h in range(2) for k in range(Y) if (h, k) != (0, 0)],
    key=lambda t: -(min(t[1], Y - t[1]) + t[0]),
)
n_row, n_chip = len(row_offsets), len(chip_offsets)


def gelu_value(value):
    inner = gelu_coef * (value + 0.044715 * value * value * value)
    return 0.5 * value * (1.0 + jnp.tanh(inner))


def gelu_slope(value):
    inner = gelu_coef * (value + 0.044715 * value * value * value)
    tanh_value = jnp.tanh(inner)
    return 0.5 * (1.0 + tanh_value) + 0.5 * value * (1.0 - tanh_value * tanh_value) * gelu_coef * (
        1.0 + 3.0 * 0.044715 * value * value
    )


def dot(left, right, left_dim, right_dim):
    return lax.dot_general(
        left, right, (((left_dim,), (right_dim,)), ((), ())), preferred_element_type=F32
    )


def pack(value):
    first, second, third = value[..., :128], value[..., 128:256], value[..., 256:]
    return jnp.concatenate(
        [jnp.concatenate([first, second], axis=-2), jnp.concatenate([third, third], axis=-2)], axis=-1
    ).astype(BF16)


def unpack(value):
    wide = value.astype(F32)
    return jnp.concatenate([wide[..., :8, :128], wide[..., 8:, :128], wide[..., :8, 128:]], axis=-1)


def kernel(
    inputs_ref, weight_in_ref, weight_out_ref, grad_ref,
    out_ref, grad_inputs_ref, grad_weight_in_ref, grad_weight_out_ref,
    eight, mine, gathered, swapped, sums, parts, hidden, product, pair_out, pair_in, chip_out, chip_in,
    send1, recv1, send_core1, recv_core1, send2, recv2, send3, recv3, send_core4, recv_core4, send4, recv4,
):
    row, col = lax.axis_index("row"), lax.axis_index("col")
    x_hi, z = row // Z, row % Z
    chip, core = col // 2, col % 2
    x_lo, y = chip // Y, chip % Y
    partner = (row, chip * 2 + 1 - core)

    def row_peer(offset, sign=1):
        return (x_hi + offset[0]) % 2, (z + sign * offset[1] + Z) % Z

    def chip_peer(offset, sign=1):
        return ((x_lo + offset[0]) % 2) * Y + (y + sign * offset[1] + Y) % Y

    barrier = pltpu.get_barrier_semaphore()
    for offset in chip_offsets:
        pl.semaphore_signal(barrier, inc=1, device_id=(row, chip_peer(offset) * 2 + core), device_id_type=MESH)
    for offset in row_offsets:
        to_x, to_z = row_peer(offset)
        pl.semaphore_signal(barrier, inc=1, device_id=(to_x * Z + to_z, col), device_id_type=MESH)
    pl.semaphore_signal(barrier, inc=1, device_id=partner, device_id_type=MESH)

    def remote(src, dst, send, recv, device):
        return pltpu.make_async_remote_copy(
            src_ref=src, dst_ref=dst, send_sem=send, recv_sem=recv, device_id=device, device_id_type=MESH
        )

    started = []

    def go(*args):
        copy = remote(*args)
        copy.start()
        started.append(copy)

    eight[0:4, :] = inputs_ref[...].astype(F32)
    eight[4:8, :] = grad_ref[...].astype(F32)
    mine[...] = pack(eight[...])
    gathered[col] = mine[...]
    pl.semaphore_wait(barrier, n_row + n_chip + 1)
    for i, offset in enumerate(chip_offsets):
        go(mine, gathered.at[col], send1.at[i], recv1.at[i], (row, chip_peer(offset) * 2 + core))
    go(mine, gathered.at[col], send_core1.at[n_chip], recv_core1.at[n_chip], partner)
    for i in reversed(range(n_chip)):
        source = chip_peer(chip_offsets[i], -1) * 2
        here = gathered.at[source + core]
        remote(mine, here, send1.at[i], recv1.at[i], partner).wait_recv()
        go(here, here, send_core1.at[i], recv_core1.at[i], partner)
    for i in reversed(range(n_chip)):
        source = chip_peer(chip_offsets[i], -1) * 2
        remote(mine, gathered.at[source + 1 - core], send_core1.at[i], recv_core1.at[i], partner).wait_recv()
    remote(mine, gathered.at[partner[1]], send_core1.at[n_chip], recv_core1.at[n_chip], partner).wait_recv()

    groups = unpack(gathered[...])
    swapped[...] = pltpu.roll(groups, 4, 1).reshape(256, 384).astype(BF16)
    stacked = groups.reshape(256, 384).astype(BF16)

    def upper(width):
        return lax.broadcasted_iota(jnp.int32, (256, width), 0) % 8 < 4

    for half in range(2):
        cut = slice(half * 384, half * 384 + 384)
        first = dot(stacked, weight_in_ref[:, cut], 1, 0)
        second = dot(stacked, weight_out_ref[cut, :], 1, 1)
        sums[half] = jnp.where(upper(384), first, second).astype(BF16).reshape(Z, 16, 384)
    for i, offset in enumerate(row_offsets):
        to_x, to_z = row_peer(offset)
        go(sums.at[to_x, to_z], parts.at[i], send2.at[i], recv2.at[i], (to_x * Z + to_z, col))
    total = sums[x_hi, z].astype(F32)
    for i in reversed(range(n_row)):
        remote(sums.at[x_hi, z], parts.at[i], send2.at[i], recv2.at[i], partner).wait_recv()
        total += parts[i].astype(F32)

    total = total.reshape(2, 8, 384)
    pre = pltpu.roll(total, 4, 1).astype(BF16).astype(F32)
    own = total.astype(BF16).astype(F32)
    act_row = lax.broadcasted_iota(jnp.int32, (2, 8, 384), 1) < 4
    hidden[x_hi, z] = jnp.where(act_row, gelu_value(own), total * gelu_slope(pre)).astype(BF16).reshape(16, 384)
    for i, offset in enumerate(row_offsets):
        to_x, to_z = row_peer(offset)
        go(hidden.at[x_hi, z], hidden.at[x_hi, z], send3.at[i], recv3.at[i], (to_x * Z + to_z, col))
    for i in reversed(range(n_row)):
        from_x, from_z = row_peer(row_offsets[i], -1)
        here = hidden.at[from_x, from_z]
        remote(here, here, send3.at[i], recv3.at[i], partner).wait_recv()

    halves = [hidden[half].reshape(256, 384) for half in range(2)]
    first = dot(halves[0], weight_out_ref[:384, :], 1, 0) + dot(halves[1], weight_out_ref[384:, :], 1, 0)
    second = dot(halves[0], weight_in_ref[:, :384], 1, 1) + dot(halves[1], weight_in_ref[:, 384:], 1, 1)
    product[...] = jnp.where(upper(384), first, second).reshape(16, 2, 8, 384)
    pair_out[...] = pack(product[:, pl.ds(1 - core, 1)].reshape(16, 8, 384))
    go(pair_out, pair_in, send_core4, recv_core4, partner)
    remote(pair_out, pair_in, send_core4, recv_core4, partner).wait_recv()
    both = product[:, pl.ds(core, 1)].reshape(16, 8, 384) + unpack(pair_in[...])
    chip_out[...] = pack(both)
    for i, offset in enumerate(chip_offsets):
        to = chip_peer(offset)
        go(chip_out.at[to], chip_in.at[i], send4.at[i], recv4.at[i], (row, to * 2 + core))

    for half in range(2):
        cut = slice(half * 384, half * 384 + 384)
        here = halves[half]
        act = jnp.where(upper(384), here.astype(F32), 0.0).astype(BF16)
        grad_pre = jnp.where(upper(384), 0.0, here.astype(F32)).astype(BF16)
        grad_weight_out_ref[cut, :] = dot(act, swapped[...], 0, 0).astype(BF16)
        grad_weight_in_ref[:, cut] = dot(swapped[...], grad_pre, 0, 0).astype(BF16)

    result = unpack(chip_out[chip])
    for i in reversed(range(n_chip)):
        remote(chip_out.at[chip], chip_in.at[i], send4.at[i], recv4.at[i], partner).wait_recv()
        result += unpack(chip_in[i])
    eight[...] = result
    out_ref[...] = eight[0:4, :].astype(BF16)
    grad_inputs_ref[...] = eight[4:8, :].astype(BF16)
    for copy in started:
        copy.wait_send()


def local(inputs, weight_in, weight_out, grad_out):
    vmem = pl.BlockSpec(memory_space=pltpu.VMEM)
    dma = pltpu.SemaphoreType.DMA
    return pl.pallas_call(
        kernel,
        out_shape=(
            jax.ShapeDtypeStruct(inputs.shape, BF16),
            jax.ShapeDtypeStruct(inputs.shape, BF16),
            jax.ShapeDtypeStruct(weight_in.shape, BF16),
            jax.ShapeDtypeStruct(weight_out.shape, BF16),
        ),
        in_specs=[vmem] * 4,
        out_specs=[vmem] * 4,
        scratch_shapes=[
            pltpu.VMEM((8, 384), F32),
            pltpu.VMEM((16, 256), BF16),
            pltpu.VMEM((32, 16, 256), BF16),
            pltpu.VMEM((256, 384), BF16),
            pltpu.VMEM((2, Z, 16, 384), BF16),
            pltpu.VMEM((n_row, 16, 384), BF16),
            pltpu.VMEM((2, Z, 16, 384), BF16),
            pltpu.VMEM((16, 2, 8, 384), F32),
            pltpu.VMEM((16, 16, 256), BF16),
            pltpu.VMEM((16, 16, 256), BF16),
            pltpu.VMEM((16, 16, 256), BF16),
            pltpu.VMEM((n_chip, 16, 256), BF16),
            dma((n_chip,)), dma((n_chip,)), dma((n_chip + 1,)), dma((n_chip + 1,)),
            dma((n_row,)), dma((n_row,)), dma((n_row,)), dma((n_row,)),
            dma, dma, dma((n_chip,)), dma((n_chip,)),
        ],
        compiler_params=pltpu.CompilerParams(
            collective_id=0, has_side_effects=True, vmem_limit_bytes=32 * 2**20
        ),
    )(inputs, weight_in, weight_out, grad_out)


def solution(mesh):
    placed = (P("col", "row"), P("row", "col"), P("col", "row"), P("col", "row"))
    return jax.shard_map(
        local,
        mesh=mesh,
        in_specs=placed,
        out_specs=(P("col", "row"), P("col", "row"), P("row", "col"), P("col", "row")),
        check_vma=False,
    )
```

```python
import functools
import math

import jax
import jax.numpy as jnp
from jax import lax
from jax.experimental import pallas as pl
from jax.experimental.pallas import tpu as pltpu
from jax.sharding import PartitionSpec as P

MESH = pl.DeviceIdType.MESH
F32, BF16 = jnp.float32, jnp.bfloat16
gelu_coef = math.sqrt(2.0 / math.pi)
Z, Y = 16, 8

cuts = ((0, 256), (256, 128))
n_cut = len(cuts)


def far_offsets(near):
    return [Z // 2] + [k for d in range(Z // 2 - 1, near, -1) for k in (d, Z - d)]


def near_offsets(near):
    return [k for d in range(near, 0, -1) for k in (d, Z - d)]


near_sum, near_send = 2, 2
chip_offsets = sorted(
    [(h, k) for h in range(2) for k in range(Y) if (h, k) != (0, 0)],
    key=lambda t: -(min(t[1], Y - t[1]) + t[0]),
)
n_chip = len(chip_offsets)
n_row = 31


def gelu_value(value):
    inner = gelu_coef * (value + 0.044715 * value * value * value)
    return 0.5 * value * (1.0 + jnp.tanh(inner))


def gelu_slope(value):
    inner = gelu_coef * (value + 0.044715 * value * value * value)
    tanh_value = jnp.tanh(inner)
    return 0.5 * (1.0 + tanh_value) + 0.5 * value * (1.0 - tanh_value * tanh_value) * gelu_coef * (
        1.0 + 3.0 * 0.044715 * value * value
    )


def dot(left, right, left_dim, right_dim):
    return lax.dot_general(
        left, right, (((left_dim,), (right_dim,)), ((), ())), preferred_element_type=F32
    )


def pack(value):
    first, second, third = value[..., :128], value[..., 128:256], value[..., 256:]
    return jnp.concatenate(
        [jnp.concatenate([first, second], axis=-2), jnp.concatenate([third, third], axis=-2)], axis=-1
    ).astype(BF16)


def unpack(value):
    wide = value.astype(F32)
    return jnp.concatenate([wide[..., :8, :128], wide[..., 8:, :128], wide[..., :8, 128:]], axis=-1)


def mix(first, second):
    low = lax.broadcasted_iota(jnp.int32, first.shape, 1) < 4
    return (
        jnp.where(low, first, pltpu.roll(second, 4, 1)),
        jnp.where(low, pltpu.roll(first, 4, 1), second),
    )


def kernel(
    inputs_hbm, weight_in_hbm, weight_out_hbm, grad_hbm,
    out_hbm, grad_inputs_hbm, grad_weight_in_hbm, grad_weight_out_hbm,
    out_ref, grad_inputs_ref, grad_weight_in_ref, grad_weight_out_ref,
    inputs_ref, weight_in_ref, weight_out_ref, grad_ref,
    eight, mine, gathered, tokens, spread, product, pair_in, chip_out, chip_in, *rest,
):
    per_cut = [rest[6 * p : 6 * p + 6] for p in range(n_cut)]
    (
        fetch, keep, entered, send1, recv1, send_core1, recv_core1, send_x2, recv_x2, send2, recv2,
        send3, recv3, send_x3, recv_x3, send_core4, recv_core4, send4, recv4,
    ) = rest[6 * n_cut :]
    row, col = lax.axis_index("row"), lax.axis_index("col")
    x_hi, z = row // Z, row % Z
    chip, core = col // 2, col % 2
    x_lo, y = chip // Y, chip % Y
    partner = (row, chip * 2 + 1 - core)
    opposite = ((1 - x_hi) * Z + z, col)

    def at_z(offset):
        return (z + offset) % Z

    def own_plane(offset):
        return (x_hi * Z + at_z(offset), col)

    def other_plane(offset):
        return ((1 - x_hi) * Z + at_z(offset), col)

    def chip_peer(offset, sign=1):
        return ((x_lo + offset[0]) % 2) * Y + (y + sign * offset[1] + Y) % Y

    def greet(semaphore, device):
        pl.semaphore_signal(semaphore, inc=1, device_id=device, device_id_type=MESH)

    barrier = pltpu.get_barrier_semaphore()
    for offset in chip_offsets:
        greet(barrier, (row, chip_peer(offset) * 2 + core))
    near_own, near_other = near_offsets(4), near_offsets(max(near_sum, near_send)) + [0]
    for offset in near_own:
        greet(barrier, own_plane(offset))
    for offset in near_other:
        greet(barrier, other_plane(offset))
    greet(barrier, partner)

    fetches = [
        pltpu.make_async_copy(src, dst, fetch.at[i])
        for i, (src, dst) in enumerate((
            (inputs_hbm, inputs_ref), (grad_hbm, grad_ref), (weight_in_hbm, weight_in_ref), (weight_out_hbm, weight_out_ref),
        ))
    ]
    for copy in fetches:
        copy.start()

    def remote(src, dst, send, recv, device):
        return pltpu.make_async_remote_copy(
            src_ref=src, dst_ref=dst, send_sem=send, recv_sem=recv, device_id=device, device_id_type=MESH
        )

    started = []

    def go(*args):
        copy = remote(*args)
        copy.start()
        started.append(copy)

    fetches[0].wait()
    fetches[1].wait()
    eight[0:4, :] = inputs_ref[...].astype(F32)
    eight[4:8, :] = grad_ref[...].astype(F32)
    mine[...] = pack(eight[...])
    place = core * 16 + chip
    gathered[place] = mine[...]
    pl.semaphore_wait(barrier, n_chip + len(near_own) + len(near_other) + 1)
    for i, offset in enumerate(chip_offsets):
        go(mine, gathered.at[place], send1.at[i], recv1.at[i], (row, chip_peer(offset) * 2 + core))
    go(mine, gathered.at[place], send_core1.at[n_chip], recv_core1.at[n_chip], partner)
    for offset in (4, 12):
        greet(entered, own_plane(offset))
    for i in reversed(range(n_chip)):
        here = gathered.at[core * 16 + chip_peer(chip_offsets[i], -1)]
        remote(mine, here, send1.at[i], recv1.at[i], partner).wait_recv()
        go(here, here, send_core1.at[i], recv_core1.at[i], partner)
    for i in reversed(range(n_chip)):
        there = gathered.at[(1 - core) * 16 + chip_peer(chip_offsets[i], -1)]
        remote(mine, there, send_core1.at[i], recv_core1.at[i], partner).wait_recv()
    there = gathered.at[(1 - core) * 16 + chip]
    remote(mine, there, send_core1.at[n_chip], recv_core1.at[n_chip], partner).wait_recv()

    groups = unpack(gathered[...])
    for i, value in enumerate(mix(groups[:16], groups[16:])):
        tokens[i] = value.reshape(128, 384).astype(BF16)
    fetches[2].wait()
    fetches[3].wait()

    far_sum, close_sum = far_offsets(near_sum), near_offsets(near_sum)
    n_far_sum = len(far_sum)

    def columns(half, p):
        return pl.ds(pl.multiple_of(half * 384 + cuts[p][0], 128), cuts[p][1])

    def hidden_sums(half, p):
        width = cuts[p][1]
        first = dot(tokens[0], weight_in_ref[:, columns(half, p)], 1, 0).reshape(16, 8, width)
        second = dot(tokens[1], weight_out_ref[columns(half, p), :], 1, 1).reshape(16, 8, width)
        return [value.reshape(8, 16, width) for value in mix(first, second)]

    for p, (sums, own_sums, crossed, passed, parts, hidden) in enumerate(per_cut):
        for i, value in enumerate(hidden_sums(1 - x_hi, p)):
            sums[0, 8 * i : 8 * i + 8] = value.astype(BF16)
        for i, offset in enumerate(far_sum):
            go(sums.at[0, at_z(offset)], crossed.at[i], send_x2.at[p, i], recv_x2.at[p, i], opposite)
        for i, offset in enumerate(close_sum + [0]):
            j = Z - 1 + i
            go(sums.at[0, at_z(offset)], parts.at[j], send2.at[p, j], recv2.at[p, j], other_plane(offset))
    for p, (sums, own_sums, crossed, passed, parts, hidden) in enumerate(per_cut):
        for i, value in enumerate(hidden_sums(x_hi, p)):
            own_sums[8 * i : 8 * i + 8] = value
            sums[1, 8 * i : 8 * i + 8] = value.astype(BF16)
        for i, offset in enumerate(close_sum):
            j = n_far_sum + i
            go(sums.at[1, at_z(offset)], parts.at[j], send2.at[p, j], recv2.at[p, j], own_plane(offset))
    pl.semaphore_wait(entered, 2)
    for p, (sums, own_sums, crossed, passed, parts, hidden) in enumerate(per_cut):
        for i, offset in enumerate(far_sum):
            remote(sums.at[0, z], crossed.at[i], send_x2.at[p, i], recv_x2.at[p, i], opposite).wait_recv()
            passed[i] = (own_sums[at_z(offset)] + crossed[i].astype(F32)).astype(BF16)
            go(passed.at[i], parts.at[i], send2.at[p, i], recv2.at[p, i], own_plane(offset))

    far_send, close_send = far_offsets(near_send), near_offsets(near_send)
    n_far_send = len(far_send)
    for p, (sums, own_sums, crossed, passed, parts, hidden) in enumerate(per_cut):
        width = cuts[p][1]
        total = own_sums[z]
        for j in reversed(range(n_far_sum, Z + len(close_sum))):
            remote(sums.at[0, z], parts.at[j], send2.at[p, j], recv2.at[p, j], opposite).wait_recv()
            total += parts[j].astype(F32)
        for j in reversed(range(n_far_sum)):
            remote(sums.at[0, z], parts.at[j], send2.at[p, j], recv2.at[p, j], opposite).wait_recv()
            total += parts[j].astype(F32)
        total = total.reshape(2, 8, width)
        pre = pltpu.roll(total, 4, 1).astype(BF16).astype(F32)
        own = total.astype(BF16).astype(F32)
        act_row = lax.broadcasted_iota(jnp.int32, total.shape, 1) < 4
        value = jnp.where(act_row, gelu_value(own), total * gelu_slope(pre))
        hidden[x_hi, z] = value.astype(BF16).reshape(16, width)
        block = hidden.at[x_hi, z]
        for i, offset in enumerate(far_send + close_send):
            go(block, block, send3.at[p, i], recv3.at[p, i], own_plane(offset))
        for i, offset in enumerate(close_send + [0]):
            j = Z - 1 + i
            go(block, block, send3.at[p, j], recv3.at[p, j], other_plane(offset))
    for p in range(n_cut):
        hidden = per_cut[p][5]
        for i in reversed(range(n_far_send)):
            here = hidden.at[x_hi, at_z(Z - far_send[i])]
            remote(here, here, send3.at[p, i], recv3.at[p, i], opposite).wait_recv()
            go(here, here, send_x3.at[p, i], recv_x3.at[p, i], opposite)

    def model_sums(half, p):
        width = cuts[p][1]
        value = per_cut[p][5][half].astype(F32).reshape(32, 8, width)
        act, grad_pre = [t.reshape(128, width).astype(BF16) for t in mix(value[:16], value[16:])]
        spread[0, :, columns(half, p)] = act
        spread[1, :, columns(half, p)] = grad_pre
        return dot(act, weight_out_ref[columns(half, p), :], 1, 0), dot(grad_pre, weight_in_ref[:, columns(half, p)], 1, 1)

    first = second = 0.0
    for p in range(n_cut):
        hidden = per_cut[p][5]
        for i, offset in enumerate(close_send):
            here = hidden.at[x_hi, at_z(Z - offset)]
            j = n_far_send + i
            remote(here, here, send3.at[p, j], recv3.at[p, j], opposite).wait_recv()
        more = model_sums(x_hi, p)
        first, second = first + more[0], second + more[1]
    for p in range(n_cut):
        hidden = per_cut[p][5]
        for i, offset in enumerate(close_send + [0]):
            j = Z - 1 + i
            there = hidden.at[1 - x_hi, at_z(Z - offset)]
            remote(there, there, send3.at[p, j], recv3.at[p, j], opposite).wait_recv()
        for i in reversed(range(n_far_send)):
            there = hidden.at[1 - x_hi, at_z(Z - far_send[i])]
            remote(there, there, send_x3.at[p, i], recv_x3.at[p, i], opposite).wait_recv()
        more = model_sums(1 - x_hi, p)
        first, second = first + more[0], second + more[1]
    for i, value in enumerate(mix(first.reshape(16, 8, 384), second.reshape(16, 8, 384))):
        product[i] = value
    go(product.at[1 - core], pair_in, send_core4, recv_core4, partner)
    remote(product.at[0], pair_in, send_core4, recv_core4, partner).wait_recv()
    chip_out[...] = pack(product[core] + pair_in[...])
    for i, offset in enumerate(chip_offsets):
        to = chip_peer(offset)
        go(chip_out.at[to], chip_in.at[i], send4.at[i], recv4.at[i], (row, to * 2 + core))

    grad_weight_out_ref[...] = dot(spread[0], tokens[1], 0, 0).astype(BF16)
    grad_weight_in_ref[...] = dot(tokens[0], spread[1], 0, 0).astype(BF16)
    kept = [
        pltpu.make_async_copy(src, dst, keep.at[i])
        for i, (src, dst) in enumerate((
            (grad_weight_in_ref, grad_weight_in_hbm), (grad_weight_out_ref, grad_weight_out_hbm),
            (out_ref, out_hbm), (grad_inputs_ref, grad_inputs_hbm),
        ))
    ]
    kept[0].start()
    kept[1].start()
    result = product[core, chip] + pair_in[chip]
    for i in reversed(range(n_chip)):
        remote(chip_out.at[chip], chip_in.at[i], send4.at[i], recv4.at[i], partner).wait_recv()
        result += unpack(chip_in[i])
    eight[...] = result
    out_ref[...] = eight[0:4, :].astype(BF16)
    grad_inputs_ref[...] = eight[4:8, :].astype(BF16)
    kept[2].start()
    kept[3].start()
    for copy in started:
        copy.wait_send()
    for copy in kept:
        copy.wait()


def store(*refs):
    sources, targets, held, load, done = refs[:4], refs[4:8], refs[8:12], refs[12], refs[13]
    order = (2, 3, 0, 1)
    loads = [pltpu.make_async_copy(sources[i], held[i], load.at[i]) for i in order]
    copies = [pltpu.make_async_copy(held[i], targets[i], done.at[i]) for i in order]
    for copy in loads:
        copy.start()
    for first, second in zip(loads, copies):
        first.wait()
        second.start()
    for copy in copies:
        copy.wait()


def local(inputs, weight_in, weight_out, grad_out):
    hbm = pl.BlockSpec(memory_space=pltpu.HBM)
    dma = pltpu.SemaphoreType.DMA
    shapes = tuple(
        jax.ShapeDtypeStruct(a.shape, BF16) for a in (inputs, inputs, weight_in, weight_out)
    )
    whole = [pltpu.VMEM(a.shape, BF16) for a in shapes]
    per_cut = []
    for _, width in cuts:
        n_far = len(far_offsets(near_sum))
        per_cut += [
            pltpu.VMEM((2, Z, 16, width), BF16),
            pltpu.VMEM((Z, 16, width), F32),
            pltpu.VMEM((n_far, 16, width), BF16),
            pltpu.VMEM((n_far, 16, width), BF16),
            pltpu.VMEM((n_row, 16, width), BF16),
            pltpu.VMEM((2, Z, 16, width), BF16),
        ]
    far = (n_cut, len(far_offsets(near_sum))), (n_cut, len(far_offsets(near_send)))
    results = pl.pallas_call(
        kernel,
        out_shape=shapes,
        in_specs=[hbm] * 4,
        out_specs=[hbm] * 4,
        scratch_shapes=[
            *whole,
            *[pltpu.VMEM(a.shape, BF16) for a in (inputs, weight_in, weight_out, grad_out)],
            pltpu.VMEM((8, 384), F32),
            pltpu.VMEM((16, 256), BF16),
            pltpu.VMEM((32, 16, 256), BF16),
            pltpu.VMEM((2, 128, 384), BF16),
            pltpu.VMEM((2, 128, 768), BF16),
            pltpu.VMEM((2, 16, 8, 384), F32),
            pltpu.VMEM((16, 8, 384), F32),
            pltpu.VMEM((16, 16, 256), BF16),
            pltpu.VMEM((n_chip, 16, 256), BF16),
            *per_cut,
            dma((4,)), dma((4,)), pltpu.SemaphoreType.REGULAR,
            dma((n_chip,)), dma((n_chip,)), dma((n_chip + 1,)), dma((n_chip + 1,)),
            dma(far[0]), dma(far[0]), dma((n_cut, n_row)), dma((n_cut, n_row)),
            dma((n_cut, n_row)), dma((n_cut, n_row)), dma(far[1]), dma(far[1]),
            dma, dma, dma((n_chip,)), dma((n_chip,)),
        ],
        compiler_params=pltpu.CompilerParams(collective_id=0, has_side_effects=True),
    )(inputs, weight_in, weight_out, grad_out)
    return pl.pallas_call(
        store,
        out_shape=shapes,
        in_specs=[hbm] * 4,
        out_specs=[hbm] * 4,
        scratch_shapes=[*whole, dma((4,)), dma((4,))],
    )(*results)


def solution(mesh):
    placed = (P("col", "row"), P("row", "col"), P("col", "row"), P("col", "row"))
    return jax.shard_map(
        local,
        mesh=mesh,
        in_specs=placed,
        out_specs=(P("col", "row"), P("col", "row"), P("row", "col"), P("col", "row")),
        check_vma=False,
    )
```

```python
import functools
import math

import jax
import jax.numpy as jnp
from jax import lax
from jax.experimental import pallas as pl
from jax.experimental.pallas import tpu as pltpu
from jax.sharding import PartitionSpec as P

MESH = pl.DeviceIdType.MESH
F32, BF16 = jnp.float32, jnp.bfloat16
gelu_coef = math.sqrt(2.0 / math.pi)
Z, Y = 16, 8

cuts = ((0, 128), (128, 256))
n_cut = len(cuts)


def far_offsets(near):
    return [Z // 2] + [k for d in range(Z // 2 - 1, near, -1) for k in (d, Z - d)]


def near_offsets(near):
    return [k for d in range(near, 0, -1) for k in (d, Z - d)]


near_sum = 0
n_first = 4
chip_offsets = sorted(
    [(h, k) for h in range(2) for k in range(Y) if (h, k) != (0, 0)],
    key=lambda t: -(min(t[1], Y - t[1]) + t[0]),
)
n_chip = len(chip_offsets)
n_row = 31


def gelu_value(value):
    inner = gelu_coef * (value + 0.044715 * value * value * value)
    return 0.5 * value * (1.0 + jnp.tanh(inner))


def gelu_slope(value):
    inner = gelu_coef * (value + 0.044715 * value * value * value)
    tanh_value = jnp.tanh(inner)
    return 0.5 * (1.0 + tanh_value) + 0.5 * value * (1.0 - tanh_value * tanh_value) * gelu_coef * (
        1.0 + 3.0 * 0.044715 * value * value
    )


def dot(left, right, left_dim, right_dim):
    return lax.dot_general(
        left, right, (((left_dim,), (right_dim,)), ((), ())), preferred_element_type=F32
    )


def pack(value):
    first, second, third = value[..., :128], value[..., 128:256], value[..., 256:]
    return jnp.concatenate(
        [jnp.concatenate([first, second], axis=-2), jnp.concatenate([third, third], axis=-2)], axis=-1
    ).astype(BF16)


def unpack(value):
    wide = value.astype(F32)
    return jnp.concatenate([wide[..., :8, :128], wide[..., 8:, :128], wide[..., :8, 128:]], axis=-1)


def mix(first, second):
    low = lax.broadcasted_iota(jnp.int32, first.shape, 1) < 4
    return (
        jnp.where(low, first, pltpu.roll(second, 4, 1)),
        jnp.where(low, pltpu.roll(first, 4, 1), second),
    )


def kernel(
    inputs_hbm, weight_in_hbm, weight_out_hbm, grad_hbm,
    out_hbm, grad_inputs_hbm, grad_weight_in_hbm, grad_weight_out_hbm,
    out_ref, grad_inputs_ref, grad_weight_in_ref, grad_weight_out_ref,
    inputs_ref, weight_in_ref, weight_out_ref, grad_ref,
    eight, mine, gathered, tokens, spread, product, pair_in, chip_out, chip_in, *rest,
):
    per_cut = [rest[6 * p : 6 * p + 6] for p in range(n_cut)]
    (
        fetch, keep, entered, send1, recv1, send_core1, recv_core1, send_x2, recv_x2, send2, recv2,
        send3, recv3, send_x3, recv_x3, send_core4, recv_core4, send4, recv4,
    ) = rest[6 * n_cut :]
    row, col = lax.axis_index("row"), lax.axis_index("col")
    x_hi, z = row // Z, row % Z
    chip, core = col // 2, col % 2
    x_lo, y = chip // Y, chip % Y
    partner = (row, chip * 2 + 1 - core)
    opposite = ((1 - x_hi) * Z + z, col)

    def at_z(offset):
        return (z + offset) % Z

    def own_plane(offset):
        return (x_hi * Z + at_z(offset), col)

    def other_plane(offset):
        return ((1 - x_hi) * Z + at_z(offset), col)

    def chip_peer(offset, sign=1):
        return ((x_lo + offset[0]) % 2) * Y + (y + sign * offset[1] + Y) % Y

    def greet(semaphore, device):
        pl.semaphore_signal(semaphore, inc=1, device_id=device, device_id_type=MESH)

    barrier = pltpu.get_barrier_semaphore()
    for offset in chip_offsets:
        greet(barrier, (row, chip_peer(offset) * 2 + core))
    near_own, near_other = near_offsets(4), near_offsets(near_sum) + [0]
    for offset in near_own:
        greet(barrier, own_plane(offset))
    for offset in near_other:
        greet(barrier, other_plane(offset))
    greet(barrier, partner)

    fetches = [
        pltpu.make_async_copy(src, dst, fetch.at[i])
        for i, (src, dst) in enumerate((
            (inputs_hbm, inputs_ref), (grad_hbm, grad_ref), (weight_in_hbm, weight_in_ref), (weight_out_hbm, weight_out_ref),
        ))
    ]
    for copy in fetches:
        copy.start()

    def remote(src, dst, send, recv, device):
        return pltpu.make_async_remote_copy(
            src_ref=src, dst_ref=dst, send_sem=send, recv_sem=recv, device_id=device, device_id_type=MESH
        )

    started = []

    def go(*args):
        copy = remote(*args)
        copy.start()
        started.append(copy)

    fetches[0].wait()
    fetches[1].wait()
    eight[0:4, :] = inputs_ref[...].astype(F32)
    eight[4:8, :] = grad_ref[...].astype(F32)
    mine[...] = pack(eight[...])
    place = core * 16 + chip
    gathered[place] = mine[...]
    pl.semaphore_wait(barrier, n_chip + len(near_own) + len(near_other) + 1)
    for i, offset in enumerate(chip_offsets):
        go(mine, gathered.at[place], send1.at[i], recv1.at[i], (row, chip_peer(offset) * 2 + core))
    go(mine, gathered.at[place], send_core1.at[n_chip], recv_core1.at[n_chip], partner)
    for offset in (4, 12):
        greet(entered, own_plane(offset))
    for i in reversed(range(n_chip)):
        here = gathered.at[core * 16 + chip_peer(chip_offsets[i], -1)]
        remote(mine, here, send1.at[i], recv1.at[i], partner).wait_recv()
        go(here, here, send_core1.at[i], recv_core1.at[i], partner)
    for i in reversed(range(n_chip)):
        there = gathered.at[(1 - core) * 16 + chip_peer(chip_offsets[i], -1)]
        remote(mine, there, send_core1.at[i], recv_core1.at[i], partner).wait_recv()
    there = gathered.at[(1 - core) * 16 + chip]
    remote(mine, there, send_core1.at[n_chip], recv_core1.at[n_chip], partner).wait_recv()

    groups = unpack(gathered[...])
    for i, value in enumerate(mix(groups[:16], groups[16:])):
        tokens[i] = value.reshape(128, 384).astype(BF16)
    fetches[2].wait()
    fetches[3].wait()

    far_sum, close_sum = far_offsets(near_sum), near_offsets(near_sum)
    n_far_sum = len(far_sum)

    def columns(half, p):
        return pl.ds(pl.multiple_of(half * 384 + cuts[p][0], 128), cuts[p][1])

    def hidden_sums(half, p):
        width = cuts[p][1]
        first = dot(tokens[0], weight_in_ref[:, columns(half, p)], 1, 0).reshape(16, 8, width)
        second = dot(tokens[1], weight_out_ref[columns(half, p), :], 1, 1).reshape(16, 8, width)
        return [value.reshape(8, 16, width) for value in mix(first, second)]

    for p, (sums, own_sums, crossed, passed, parts, hidden) in enumerate(per_cut):
        for i, value in enumerate(hidden_sums(1 - x_hi, p)):
            sums[0, 8 * i : 8 * i + 8] = value.astype(BF16)
        for i, offset in enumerate(far_sum):
            go(sums.at[0, at_z(offset)], crossed.at[i], send_x2.at[p, i], recv_x2.at[p, i], opposite)
        for i, offset in enumerate(close_sum + [0]):
            j = Z - 1 + i
            go(sums.at[0, at_z(offset)], parts.at[j], send2.at[p, j], recv2.at[p, j], other_plane(offset))
    for p, (sums, own_sums, crossed, passed, parts, hidden) in enumerate(per_cut):
        for i, value in enumerate(hidden_sums(x_hi, p)):
            own_sums[8 * i : 8 * i + 8] = value
            sums[1, 8 * i : 8 * i + 8] = value.astype(BF16)
        for i, offset in enumerate(close_sum):
            j = n_far_sum + i
            go(sums.at[1, at_z(offset)], parts.at[j], send2.at[p, j], recv2.at[p, j], own_plane(offset))
    pl.semaphore_wait(entered, 2)
    for p, (sums, own_sums, crossed, passed, parts, hidden) in enumerate(per_cut):
        for i, offset in enumerate(far_sum):
            remote(sums.at[0, z], crossed.at[i], send_x2.at[p, i], recv_x2.at[p, i], opposite).wait_recv()
            passed[i] = (own_sums[at_z(offset)] + crossed[i].astype(F32)).astype(BF16)
            go(passed.at[i], parts.at[i], send2.at[p, i], recv2.at[p, i], own_plane(offset))

    far_send = far_offsets(0)

    def send_hidden(p, offset):
        block = per_cut[p][5].at[x_hi, z]
        remote(block, block, send3.at[p, offset], recv3.at[p, offset], own_plane(offset)).start()

    for p, (sums, own_sums, crossed, passed, parts, hidden) in enumerate(per_cut):
        width = cuts[p][1]
        total = own_sums[z]
        for j in reversed(range(n_far_sum, Z + len(close_sum))):
            remote(sums.at[0, z], parts.at[j], send2.at[p, j], recv2.at[p, j], opposite).wait_recv()
            total += parts[j].astype(F32)
        for j in reversed(range(n_far_sum)):
            remote(sums.at[0, z], parts.at[j], send2.at[p, j], recv2.at[p, j], opposite).wait_recv()
            total += parts[j].astype(F32)
        total = total.reshape(2, 8, width)
        pre = pltpu.roll(total, 4, 1).astype(BF16).astype(F32)
        own = total.astype(BF16).astype(F32)
        act_row = lax.broadcasted_iota(jnp.int32, total.shape, 1) < 4
        value = jnp.where(act_row, gelu_value(own), total * gelu_slope(pre))
        hidden[x_hi, z] = value.astype(BF16).reshape(16, width)
        block = hidden.at[x_hi, z]
        for target in range(n_first):
            @pl.when(z != target)
            def _():
                send_hidden(p, (target - z + Z) % Z)
        go(block, block, send3.at[p, 0], recv3.at[p, 0], opposite)
    for p in range(n_cut):
        for offset in far_send:
            @pl.when(at_z(offset) >= n_first)
            def _():
                send_hidden(p, offset)
    for p in range(n_cut):
        hidden = per_cut[p][5]
        for offset in reversed(far_send):
            here = hidden.at[x_hi, at_z(Z - offset)]
            remote(here, here, send3.at[p, offset], recv3.at[p, offset], opposite).wait_recv()
            go(here, here, send_x3.at[p, offset], recv_x3.at[p, offset], opposite)

    def model_sums(half, p):
        width = cuts[p][1]
        value = per_cut[p][5][half].astype(F32).reshape(32, 8, width)
        act, grad_pre = [t.reshape(128, width).astype(BF16) for t in mix(value[:16], value[16:])]
        spread[0, :, columns(half, p)] = act
        spread[1, :, columns(half, p)] = grad_pre
        return dot(act, weight_out_ref[columns(half, p), :], 1, 0), dot(grad_pre, weight_in_ref[:, columns(half, p)], 1, 1)

    first = second = 0.0
    for p in range(n_cut):
        more = model_sums(x_hi, p)
        first, second = first + more[0], second + more[1]
    for p in range(n_cut):
        hidden = per_cut[p][5]
        there = hidden.at[1 - x_hi, z]
        remote(there, there, send3.at[p, 0], recv3.at[p, 0], opposite).wait_recv()
        for offset in reversed(far_send):
            there = hidden.at[1 - x_hi, at_z(Z - offset)]
            remote(there, there, send_x3.at[p, offset], recv_x3.at[p, offset], opposite).wait_recv()
        more = model_sums(1 - x_hi, p)
        first, second = first + more[0], second + more[1]
    for i, value in enumerate(mix(first.reshape(16, 8, 384), second.reshape(16, 8, 384))):
        product[i] = value
    go(product.at[1 - core], pair_in, send_core4, recv_core4, partner)
    remote(product.at[0], pair_in, send_core4, recv_core4, partner).wait_recv()
    chip_out[...] = pack(product[core] + pair_in[...])
    for i, offset in enumerate(chip_offsets):
        to = chip_peer(offset)
        go(chip_out.at[to], chip_in.at[i], send4.at[i], recv4.at[i], (row, to * 2 + core))

    grad_weight_out_ref[...] = dot(spread[0], tokens[1], 0, 0).astype(BF16)
    grad_weight_in_ref[...] = dot(tokens[0], spread[1], 0, 0).astype(BF16)
    kept = [
        pltpu.make_async_copy(src, dst, keep.at[i])
        for i, (src, dst) in enumerate((
            (grad_weight_in_ref, grad_weight_in_hbm), (grad_weight_out_ref, grad_weight_out_hbm),
            (out_ref, out_hbm), (grad_inputs_ref, grad_inputs_hbm),
        ))
    ]
    kept[0].start()
    kept[1].start()
    result = product[core, chip] + pair_in[chip]
    for i in reversed(range(n_chip)):
        remote(chip_out.at[chip], chip_in.at[i], send4.at[i], recv4.at[i], partner).wait_recv()
        result += unpack(chip_in[i])
    eight[...] = result
    out_ref[...] = eight[0:4, :].astype(BF16)
    grad_inputs_ref[...] = eight[4:8, :].astype(BF16)
    kept[2].start()
    kept[3].start()
    for copy in started:
        copy.wait_send()
    for p in range(n_cut):
        for offset in far_send:
            block = per_cut[p][5].at[x_hi, z]
            remote(block, block, send3.at[p, offset], recv3.at[p, offset], opposite).wait_send()
    for copy in kept:
        copy.wait()


def store(*refs):
    sources, targets, held, load, done = refs[:4], refs[4:8], refs[8:12], refs[12], refs[13]
    order = (2, 3, 0, 1)
    loads = [pltpu.make_async_copy(sources[i], held[i], load.at[i]) for i in order]
    copies = [pltpu.make_async_copy(held[i], targets[i], done.at[i]) for i in order]
    for copy in loads:
        copy.start()
    for first, second in zip(loads, copies):
        first.wait()
        second.start()
    for copy in copies:
        copy.wait()


def local(inputs, weight_in, weight_out, grad_out):
    hbm = pl.BlockSpec(memory_space=pltpu.HBM)
    dma = pltpu.SemaphoreType.DMA
    shapes = tuple(
        jax.ShapeDtypeStruct(a.shape, BF16) for a in (inputs, inputs, weight_in, weight_out)
    )
    whole = [pltpu.VMEM(a.shape, BF16) for a in shapes]
    per_cut = []
    for _, width in cuts:
        n_far = len(far_offsets(near_sum))
        per_cut += [
            pltpu.VMEM((2, Z, 16, width), BF16),
            pltpu.VMEM((Z, 16, width), F32),
            pltpu.VMEM((n_far, 16, width), BF16),
            pltpu.VMEM((n_far, 16, width), BF16),
            pltpu.VMEM((n_row, 16, width), BF16),
            pltpu.VMEM((2, Z, 16, width), BF16),
        ]
    far = n_cut, len(far_offsets(near_sum))
    results = pl.pallas_call(
        kernel,
        out_shape=shapes,
        in_specs=[hbm] * 4,
        out_specs=[hbm] * 4,
        scratch_shapes=[
            *whole,
            *[pltpu.VMEM(a.shape, BF16) for a in (inputs, weight_in, weight_out, grad_out)],
            pltpu.VMEM((8, 384), F32),
            pltpu.VMEM((16, 256), BF16),
            pltpu.VMEM((32, 16, 256), BF16),
            pltpu.VMEM((2, 128, 384), BF16),
            pltpu.VMEM((2, 128, 768), BF16),
            pltpu.VMEM((2, 16, 8, 384), F32),
            pltpu.VMEM((16, 8, 384), F32),
            pltpu.VMEM((16, 16, 256), BF16),
            pltpu.VMEM((n_chip, 16, 256), BF16),
            *per_cut,
            dma((4,)), dma((4,)), pltpu.SemaphoreType.REGULAR,
            dma((n_chip,)), dma((n_chip,)), dma((n_chip + 1,)), dma((n_chip + 1,)),
            dma(far), dma(far), dma((n_cut, n_row)), dma((n_cut, n_row)),
            dma((n_cut, Z)), dma((n_cut, Z)), dma((n_cut, Z)), dma((n_cut, Z)),
            dma, dma, dma((n_chip,)), dma((n_chip,)),
        ],
        compiler_params=pltpu.CompilerParams(collective_id=0, has_side_effects=True),
    )(inputs, weight_in, weight_out, grad_out)
    return pl.pallas_call(
        store,
        out_shape=shapes,
        in_specs=[hbm] * 4,
        out_specs=[hbm] * 4,
        scratch_shapes=[*whole, dma((4,)), dma((4,))],
    )(*results)


def solution(mesh):
    placed = (P("col", "row"), P("row", "col"), P("col", "row"), P("col", "row"))
    return jax.shard_map(
        local,
        mesh=mesh,
        in_specs=placed,
        out_specs=(P("col", "row"), P("col", "row"), P("row", "col"), P("col", "row")),
        check_vma=False,
    )
```
